256 devices in a mesh: seq: 64 (over y, z, core), fsdp: 4 (over x).
Axes of the slice: x: 4, y: 4, z: 8, core: 2. Of those that a mesh axis runs over, the one named last changes fastest.
Arguments:
- queries: bfloat16 [16384, 2048], P('seq', 'fsdp'), may hold values from -2.5 to 2.5
- keys_values: bfloat16 [16384, 512], P('seq', 'fsdp'), may hold values from -2.5 to 2.5
- hidden_in: bfloat16 [16384, 2880], P(('seq', 'fsdp')), may hold values from -6 to 6
- out_weight: bfloat16 [2048, 2880], P('fsdp'), may hold values from -0.5 to 0.5
- norm_gain: float32 [2880], replicated, may hold values from 0.1 to 1.9
- router_weight: bfloat16 [2880, 64], replicated, may hold values from -0.109375 to 0.109375
- expert_ids: int32 [16384, 4], P(('seq', 'fsdp')), may hold values from 0 to 63, all different within a row; in each aligned block of 64 rows (0 to 63, 64 to 127, ...) at most 8 rows name the same one
- expert_gate: bfloat16 [64, 2880, 1536], P('seq', None, 'fsdp'), may hold values from -0.109375 to 0.109375
- expert_up: bfloat16 [64, 2880, 1536], P('seq', None, 'fsdp'), may hold values from -0.109375 to 0.109375
- expert_down: bfloat16 [64, 2880, 1536], P('seq', None, 'fsdp'), may hold values from -0.15625 to 0.15625
Outputs:
- layer_out: bfloat16 [16384, 2880], P(('seq', 'fsdp'))
The draws below stay inside these ranges and needn't reach their ends.
Inputs may be any that keep to these rules, and one draw needn't show every extreme that they name: `expert_ids`: A row names 4 different experts. Within the rows of one device (aligned blocks of 64 rows) no expert is named by more than 8 rows, a bound that some block reaches.
All inputs are finite; a program needn't handle non-finite values.
Results may differ from the reference program's by a relative error of at most 0.0075.
Values may be sent and summed in bfloat16 or wider, within the bound.
No kernel may reach another device: no remote copies, remote signals or barrier semaphores. Data moves between devices by JAX's collectives and lax.ppermute only.
A program may use at most 128 MiB of HBM per device.

```python
import math
import jax
import jax.numpy as jnp
import numpy as np
from jax import lax

D = 2880
FF = 1536
HD = 64
QH = 32
KVH = 4
WINDOW = 128
TOPK = 4
TOK_DEV = 256
TOKENS = 16384
ROWS_DEV = 64
EXPERTS = 64
MOST = 8
N_FSDP = 4


def shard_levels(stream_key, dims, shards, smallest, high):
    loudness, own = 1.0, jax.random.fold_in(stream_key, 6)
    for dim, parts in shards:
        heights = jnp.exp(jax.random.uniform(jax.random.fold_in(own, dim), (parts,), jnp.float32, smallest / len(shards), high / len(shards)))
        loudness = loudness * jnp.repeat(heights, dims[dim] // parts).reshape([-1 if axis == dim else 1 for axis in range(len(dims))])
    return loudness


def shared_out(stream_key, own, number, rows, number_of, top, limit, slope):
    ranking = jax.random.permutation(stream_key, number_of)
    packed, ordinary = shares(number_of, rows * top, limit, slope, True), shares(number_of, rows * top, limit, slope, False)
    places = jnp.arange(number_of)

    def named(tallies, offset_by):
        used = int((tallies > 0).sum())
        fixed = max(1, used // 4)
        passed = fixed + (places - fixed + offset_by * (used - fixed)) % max(1, number_of - fixed)
        return jnp.zeros((number_of,), jnp.int32).at[ranking[jnp.where(places < fixed, places, passed)]].set(jnp.asarray(tallies, jnp.int32))

    tallies = jnp.where(number % 4 == 0, named(packed, number // 4), named(ordinary, number - number // 4 - 1))
    mixed = jax.random.permutation(jax.random.fold_in(own, 3), number_of)
    source_of, taker = mixed[0:number_of // 2 * 2:2], mixed[1:number_of // 2 * 2:2]
    slack = jnp.minimum(tallies[source_of] - 1, limit - tallies[taker]) // 2
    slack = jnp.where((source_of == ranking[0]) | (taker == ranking[0]) | (tallies[taker] == 0), 0, jnp.maximum(slack, 0))
    passed = jax.random.randint(jax.random.fold_in(own, 4), (number_of // 2,), 0, 1 << 20) % (slack + 1)
    tallies = tallies.at[source_of].add(-passed).at[taker].add(passed)
    labels = jnp.searchsorted(jnp.cumsum(tallies), jnp.arange(rows * top), side="right").astype(jnp.int32)
    listing = labels.reshape(top, rows).T
    listing = listing[jax.random.permutation(jax.random.fold_in(own, 1), rows)]
    offset_by = jax.random.randint(jax.random.fold_in(own, 2), (rows, 1), 0, top)
    return jnp.take_along_axis(listing, (jnp.arange(top)[None, :] + offset_by) % top, axis=1)


def shares(number_of, total, limit, lean, full):
    portions = [(1 << 20) // math.isqrt(grade ** lean) + 1 for grade in range(1, number_of + 1)]
    largest = limit if full else min(limit, max(-(-total // number_of), total * portions[0] // sum(portions)))
    least = 1 if total - largest >= number_of - 1 else 0
    holding, rest = [largest] + [least] * (number_of - 1), total - largest - least * (number_of - 1)
    while rest > 0:
        candidates = [i for i in range(1, number_of) if holding[i] < largest] or [i for i in range(1, number_of) if holding[i] < limit]
        pool, budget = sum([portions[i] for i in candidates]), rest
        for i in candidates:
            more = min(limit - holding[i], max(1, budget * portions[i] // pool), rest)
            holding[i] = holding[i] + more
            rest = rest - more
    return np.array(holding)


def scatter_about(key, dims, scale, bound, pieces=(), kind=jnp.bfloat16):
    factor_of = shard_levels(key, dims, pieces, -0.22, 0.18) if pieces else 1.0
    drawn = jax.random.normal(key, dims, jnp.float32) * scale * factor_of
    return jnp.minimum(jnp.maximum(drawn, -bound), bound).astype(kind)


def setup_inputs(seed: int = 0) -> dict:
    key_of = jax.random.split(jax.random.key(seed), 11)
    queries = scatter_about(key_of[0], (TOKENS, QH * HD), 1.0, 2.5, ((0, 64), (1, 4)))
    keys_values = scatter_about(key_of[1], (TOKENS, KVH * 2 * HD), 1.0, 2.5, ((0, 64), (1, 4)))
    hidden_in = scatter_about(key_of[2], (TOKENS, D), 1.0, 6.0, ((0, 256),))
    out_weight = scatter_about(key_of[3], (QH * HD, D), (QH * HD // 16) ** -0.5, 0.5, ((0, 4),))
    norm_gain = jnp.clip(1.0 + 0.18 * jax.random.normal(key_of[4], (D,), jnp.float32), 0.1, 1.9)
    router_weight = scatter_about(key_of[5], (D, EXPERTS), D ** -0.5, 0.109375)
    expert_ids_keys = jax.random.split(jax.random.fold_in(key_of[6], 1), TOKENS // ROWS_DEV)
    expert_ids_turns = jax.random.permutation(jax.random.fold_in(key_of[6], 3), TOKENS // ROWS_DEV)
    expert_ids = jax.vmap(lambda own, number: shared_out(jax.random.fold_in(key_of[6], 2), own, number, ROWS_DEV, EXPERTS, TOPK, MOST, 2))(expert_ids_keys, expert_ids_turns).reshape((TOKENS, TOPK))
    expert_gate = scatter_about(key_of[7], (EXPERTS, D, FF), D ** -0.5, 0.109375, ((0, 64), (2, 4)))
    expert_up = scatter_about(key_of[8], (EXPERTS, D, FF), D ** -0.5, 0.109375, ((0, 64), (2, 4)))
    expert_down = scatter_about(key_of[9], (EXPERTS, D, FF), FF ** -0.5, 0.15625, ((0, 64), (2, 4)))
    return dict(queries=queries, keys_values=keys_values, hidden_in=hidden_in, out_weight=out_weight, norm_gain=norm_gain, router_weight=router_weight, expert_ids=expert_ids, expert_gate=expert_gate, expert_up=expert_up, expert_down=expert_down)


def reference(queries, keys_values, hidden_in, out_weight, norm_gain, router_weight, expert_ids, expert_gate, expert_up, expert_down):
    score_scale = 1.0 / math.sqrt(HD)
    groups = QH // KVH
    padded_kv = jnp.concatenate([jnp.zeros((WINDOW, KVH * 2 * HD), keys_values.dtype), keys_values], axis=0)

    def one_block(block_num):
        first_row = block_num * TOK_DEV
        query_rows = lax.dynamic_slice_in_dim(queries, first_row, TOK_DEV, 0).astype(jnp.float32).reshape(TOK_DEV, KVH, groups, HD)
        kv_rows = lax.dynamic_slice_in_dim(padded_kv, first_row, WINDOW + TOK_DEV, 0).astype(jnp.float32).reshape(WINDOW + TOK_DEV, KVH, 2, HD)
        scores = jnp.einsum('tkgd,skd->kgts', query_rows, kv_rows[:, :, 0]) * score_scale
        query_pos = first_row + jnp.arange(TOK_DEV, dtype=jnp.int32)
        key_pos = first_row - WINDOW + jnp.arange(WINDOW + TOK_DEV, dtype=jnp.int32)
        offset = query_pos[:, None] - key_pos[None, :]
        allowed = (offset >= 0) & (offset <= WINDOW) & (key_pos[None, :] >= 0)
        raised = jnp.where(allowed, jnp.exp(scores), 0.0)
        attn_probs = (raised / lax.optimization_barrier(jnp.sum(raised, axis=-1, keepdims=True))).astype(jnp.bfloat16)
        mixed_heads = jnp.einsum('kgts,skd->tkgd', attn_probs.astype(jnp.float32), kv_rows[:, :, 1])
        return mixed_heads.astype(jnp.bfloat16).reshape(TOK_DEV, QH * HD)
    attended = lax.map(one_block, jnp.arange(TOKENS // TOK_DEV, dtype=jnp.int32)).reshape(TOKENS, QH * HD)
    projected = jnp.dot(attended, out_weight, preferred_element_type=jnp.float32)
    stream = (hidden_in.astype(jnp.float32) + projected).astype(jnp.bfloat16)
    stream = lax.optimization_barrier(stream)
    stream_wide = stream.astype(jnp.float32)
    inverse = lax.rsqrt(lax.optimization_barrier(jnp.mean(stream_wide * stream_wide, axis=1, keepdims=True)) + 1e-05)
    normed = (stream_wide * inverse * norm_gain).astype(jnp.bfloat16)
    logits = jnp.dot(normed, router_weight, preferred_element_type=jnp.float32)
    chosen = expert_ids[:, :, None] == jnp.arange(EXPERTS, dtype=jnp.int32)[None, None, :]
    picked = lax.optimization_barrier(jnp.sum(jnp.where(chosen, logits[:, None, :], 0.0), axis=2))
    raised_gates = jnp.exp(picked)
    gates = raised_gates / lax.optimization_barrier(jnp.sum(raised_gates, axis=1, keepdims=True))
    rows_dev = TOK_DEV // N_FSDP
    block_count = TOKENS // rows_dev
    block_ids = expert_ids.reshape(block_count, rows_dev * TOPK)
    onehot = (block_ids[:, :, None] == jnp.arange(EXPERTS, dtype=jnp.int32)[None, None, :]).astype(jnp.int32)
    running = jnp.cumsum(onehot, axis=1, dtype=jnp.int32) - onehot
    slot_ids = lax.optimization_barrier(jnp.sum(running * onehot, axis=2, dtype=jnp.int32))
    block_index = jnp.arange(block_count, dtype=jnp.int32)[:, None]
    assign_index = jnp.arange(rows_dev * TOPK, dtype=jnp.int32)[None, :]
    token_index = block_index * rows_dev + assign_index // TOPK
    position = ((block_ids * block_count + block_index) * MOST + slot_ids).reshape(-1)
    table = jnp.full((EXPERTS * block_count * MOST,), TOKENS, jnp.int32).at[position].set(token_index.reshape(-1).astype(jnp.int32))
    padded_norm = jnp.concatenate([normed, jnp.zeros((1, D), normed.dtype)], axis=0)

    def one_expert(expert_num):
        picks = lax.dynamic_slice_in_dim(table, expert_num * block_count * MOST, block_count * MOST, 0)
        row_block = padded_norm[picks]
        gate_part = jnp.dot(row_block, expert_gate[expert_num], preferred_element_type=jnp.float32)
        up_part = jnp.dot(row_block, expert_up[expert_num], preferred_element_type=jnp.float32)
        hidden = (gate_part * jax.nn.sigmoid(1.702 * gate_part) * (up_part + 1.0)).astype(jnp.bfloat16)
        return jnp.dot(hidden, expert_down[expert_num].T, preferred_element_type=jnp.float32).astype(jnp.bfloat16)
    outputs = lax.map(one_expert, jnp.arange(EXPERTS, dtype=jnp.int32)).reshape(EXPERTS * block_count * MOST, D)
    fetched = outputs[position].astype(jnp.float32).reshape(TOKENS, TOPK, D)
    expert_sum = lax.optimization_barrier(jnp.sum(fetched * gates[:, :, None], axis=1))
    return (stream_wide + expert_sum).astype(jnp.bfloat16)
```

```python
import functools
import math

import jax
import jax.numpy as jnp
from jax import lax
from jax.experimental import pallas as pl
from jax.experimental.pallas import tpu as pltpu
from jax.sharding import PartitionSpec as P

D = 2880
HD = 64
WINDOW = 128
TOPK = 4
SLOTS = 8
EXPERTS = 64
CHUNKS = 2
PER = SLOTS // CHUNKS
F32 = jnp.float32
BF16 = jnp.bfloat16
NT = (((1,), (1,)), ((), ()))
TN = (((0,), (0,)), ((), ()))
VMEM = pl.BlockSpec(memory_space=pltpu.VMEM)
SMEM = pl.BlockSpec(memory_space=pltpu.SMEM)
ANY = pl.BlockSpec(memory_space=pl.ANY)
BESIDE_WEIGHTS = [(0, 3), (3, 0), (1, 2), (2, 1)]
BESIDE_ROWS = [(0, 1), (1, 0), (2, 3), (3, 2)]


def call(body, outs, in_specs, scratch=(), flops=0, nbytes=0, limit=48):
    return pl.pallas_call(
        body,
        out_shape=outs,
        in_specs=in_specs,
        out_specs=jax.tree.map(lambda _: VMEM, outs),
        scratch_shapes=list(scratch),
        compiler_params=pltpu.CompilerParams(vmem_limit_bytes=limit << 20),
        cost_estimate=pl.CostEstimate(flops=flops, bytes_accessed=nbytes, transcendentals=0),
    )


def attention_body(place, q_ref, kv_ref, rim_ref, ow_ref, own_ref, to1, to2, to3, mixed):
    first, x = place[0] == 0, place[1]
    ext = jnp.concatenate([rim_ref[...], kv_ref[...]], axis=0)
    keys, values = ext[:, :HD], ext[:, HD:]
    row = lax.broadcasted_iota(jnp.int32, (WINDOW, 2 * WINDOW), 0)
    col = lax.broadcasted_iota(jnp.int32, (WINDOW, 2 * WINDOW), 1)
    band = (col >= row) & (col <= row + WINDOW)
    for b in range(2):
        allowed = band
        if b == 0:
            allowed = band & ((col >= WINDOW) | jnp.logical_not(first))
        k = keys[b * WINDOW : b * WINDOW + 2 * WINDOW]
        v = values[b * WINDOW : b * WINDOW + 2 * WINDOW]
        heads = []
        for h in range(q_ref.shape[1] // HD):
            q = q_ref[b * WINDOW : (b + 1) * WINDOW, h * HD : (h + 1) * HD]
            scores = lax.dot_general(q, k, NT, preferred_element_type=F32) * (1.0 / math.sqrt(HD))
            raised = jnp.where(allowed, jnp.exp(scores), 0.0)
            probs = (raised / jnp.sum(raised, axis=-1, keepdims=True)).astype(BF16)
            heads.append(jnp.dot(probs, v, preferred_element_type=F32))
        attended = jnp.concatenate(heads, axis=1).astype(BF16)
        for half in range(2):
            place_of = lax.rem(2 * b + half - x + 4, 4) * 64
            mixed[pl.ds(pl.multiple_of(place_of, 64), 64), :] = attended[half * 64 : half * 64 + 64]
    out = jnp.dot(mixed[...], ow_ref[...], preferred_element_type=F32)
    own_ref[...] = out[:64]
    to1[...] = out[64:128].astype(BF16)
    to2[...] = out[128:192].astype(BF16)
    to3[...] = out[192:].astype(BF16)


def norm_body(own, r1, r2, r3, hid, gain, pick0, pick1, stream_ref, normed_ref, out0, out1):
    projected = own[...] + r1[...].astype(F32) + r2[...].astype(F32) + r3[...].astype(F32)
    stream = (hid[...].astype(F32) + projected).astype(BF16)
    stream_ref[...] = stream
    wide = stream.astype(F32)
    inverse = lax.rsqrt(jnp.mean(wide * wide, axis=1, keepdims=True) + 1e-05)
    normed = (wide * inverse * gain[...]).astype(BF16)
    normed_ref[...] = normed
    out0[...] = jnp.dot(pick0[...], normed, preferred_element_type=F32).astype(BF16)
    out1[...] = jnp.dot(pick1[...], normed, preferred_element_type=F32).astype(BF16)


def gates_body(normed, router, chosen_t, spread, pick0, pick1, mix0, mix1):
    logits = lax.dot_general(router[...], normed[...], (((0,), (1,)), ((), ())), preferred_element_type=F32)
    raised = jnp.where(chosen_t[...] > 0.5, jnp.exp(logits), 0.0)
    gates = raised / jnp.sum(raised, axis=0, keepdims=True)
    rows = jnp.dot(spread[...], gates, preferred_element_type=F32, precision=lax.Precision.HIGHEST)
    for pick, mix in ((pick0, mix0), (pick1, mix1)):
        weight = pick[...].astype(F32) * rows
        high = weight.astype(BF16)
        low = (weight - high.astype(F32)).astype(BF16)
        mix[...] = jnp.concatenate([high, low], axis=1)


def hidden_body(xo, xp, g0, u0, g1, u1, ho, hp, vx, vw, sems):
    copies = [pltpu.make_async_copy(src, vx.at[i], sems.at[i]) for i, src in enumerate((xo, xp))]
    copies += [pltpu.make_async_copy(src, vw.at[i], sems.at[2 + i]) for i, src in enumerate((g0, u0, g1, u1))]
    for c in copies:
        c.start()
    width = g0.shape[1]
    copies[0].wait()
    copies[1].wait()
    for part in range(2):
        copies[2 + 2 * part].wait()
        copies[3 + 2 * part].wait()
        for i, h_ref in ((1, hp), (0, ho)):
            gate = jnp.dot(vx[i], vw[2 * part], preferred_element_type=F32)
            up = jnp.dot(vx[i], vw[2 * part + 1], preferred_element_type=F32)
            act = gate * jax.nn.sigmoid(1.702 * gate) * (up + 1.0)
            h_ref[:, part * width : (part + 1) * width] = act.astype(BF16)


def down_body(ho, hr, d0, d1, d2, d3, out, vw, acc, sems):
    copies = [pltpu.make_async_copy(src, vw.at[i], sems.at[i]) for i, src in enumerate((d0, d1, d2, d3))]
    for c in copies:
        c.start()
    width = d0.shape[1]
    for i in range(4):
        copies[i].wait()
        h = (ho, hr)[i // 2][:, (i % 2) * width : (i % 2 + 1) * width]
        term = lax.dot_general(h, vw[i], NT, preferred_element_type=F32)
        if i == 0:
            acc[...] = term
        elif i < 3:
            acc[...] += term
        else:
            out[...] = (acc[...] + term).astype(BF16)


def combine_body(stream, mix0, mix1, ret0, ret1, out):
    both = lax.dot_general(mix0[...], ret0[...], TN, preferred_element_type=F32)
    both += lax.dot_general(mix1[...], ret1[...], TN, preferred_element_type=F32)
    out[...] = (stream[...].astype(F32) + both[:64] + both[64:]).astype(BF16)


def shape(*dims, dtype=BF16):
    return jax.ShapeDtypeStruct(dims, dtype)


def per_device(
    queries,
    keys_values,
    hidden_in,
    out_weight,
    norm_gain,
    router_weight,
    expert_ids,
    expert_gate,
    expert_up,
    expert_down,
):
    tok_dev = queries.shape[0]
    rows_dev = hidden_in.shape[0]
    gate, up, down = expert_gate[0], expert_up[0], expert_down[0]
    width = gate.shape[1]
    owners = lax.axis_size("seq")
    rows = owners * PER

    beside_w = functools.partial(lax.ppermute, axis_name="fsdp", perm=BESIDE_WEIGHTS)
    beside_r = functools.partial(lax.ppermute, axis_name="fsdp", perm=BESIDE_ROWS)

    def shift(a, by):
        return lax.ppermute(a, "fsdp", [(i, (i + by) % 4) for i in range(4)])

    key_rim = lax.ppermute(
        keys_values[tok_dev - WINDOW :], "seq", [(i, i + 1) for i in range(owners - 1)]
    )
    gate_w, up_w = beside_w(gate), beside_w(up)
    down_r = beside_r(down)
    down_w = beside_w(down)
    far_low = beside_w(down_r[: D // 2])
    far_high = beside_r(down_w[D // 2 :])
    down_x = jnp.concatenate([far_low, far_high], axis=0)

    chosen = jnp.any(
        expert_ids[:, :, None] == jnp.arange(EXPERTS, dtype=jnp.int32)[None, None, :], axis=1
    ).astype(F32)
    before = (jnp.arange(rows_dev)[:, None] < jnp.arange(rows_dev)[None, :]).astype(F32)
    rank_t = lax.dot_general(chosen, before, TN, preferred_element_type=F32)
    chosen_t = chosen.T
    picks = []
    for c in range(CHUNKS):
        slot = (c * PER + jnp.arange(PER)).astype(F32)[None, :, None]
        hit = (chosen_t[:, None, :] > 0.5) & (rank_t[:, None, :] == slot)
        picks.append(hit.astype(BF16).reshape(rows, rows_dev))
    spread = (jnp.arange(rows)[:, None] // PER == jnp.arange(EXPERTS)[None, :]).astype(F32)

    place = jnp.stack([lax.axis_index("seq"), lax.axis_index("fsdp")]).astype(jnp.int32)
    own, to1, to2, to3 = call(
        attention_body,
        (shape(rows_dev, D, dtype=F32),) + (shape(rows_dev, D),) * 3,
        [SMEM] + [VMEM] * 4,
        [pltpu.VMEM((tok_dev, queries.shape[1]), BF16)],
        flops=2 * tok_dev * 512 * D,
        nbytes=8 << 20,
    )(place, queries, keys_values, key_rim, out_weight)
    r1, r2, r3 = shift(to1, 1), shift(to2, 2), shift(to3, 3)
    stream, normed, out0, out1 = call(
        norm_body,
        (shape(rows_dev, D), shape(rows_dev, D), shape(rows, D), shape(rows, D)),
        [VMEM] * 8,
        flops=4 * rows * rows_dev * D,
        nbytes=6 << 20,
    )(own, r1, r2, r3, hidden_in, norm_gain[None, :], *picks)

    def exchange(a):
        return lax.all_to_all(
            a.reshape(owners, PER, D), "seq", split_axis=0, concat_axis=0, tiled=True
        ).reshape(rows, D)

    received = [exchange(out0), exchange(out1)]
    mix0, mix1 = call(
        gates_body,
        (shape(rows, 2 * rows_dev),) * 2,
        [VMEM] * 6,
        flops=2 * rows_dev * D * EXPERTS,
        nbytes=1 << 20,
    )(normed, router_weight, chosen_t, spread, *picks)

    returned = []
    for mine in received:
        theirs = beside_r(mine)
        hid_mine, hid_theirs = call(
            hidden_body,
            (shape(rows, 2 * width),) * 2,
            [ANY] * 6,
            [
                pltpu.VMEM((2, rows, D), BF16),
                pltpu.VMEM((4, D, width), BF16),
                pltpu.SemaphoreType.DMA((6,)),
            ],
            flops=16 * rows * D * width,
            nbytes=12 << 20,
        )(mine, theirs, gate, up, gate_w, up_w)
        hid_rest = beside_r(hid_theirs)
        answer = call(
            down_body,
            shape(rows, D),
            [VMEM] * 2 + [ANY] * 4,
            [
                pltpu.VMEM((4, D, width), BF16),
                pltpu.VMEM((rows, D), F32),
                pltpu.SemaphoreType.DMA((4,)),
            ],
            flops=8 * rows * D * width,
            nbytes=12 << 20,
        )(hid_mine, hid_rest, down, down_w, down_r, down_x)
        returned.append(exchange(answer))
    return call(
        combine_body,
        shape(rows_dev, D),
        [VMEM] * 5,
        flops=8 * rows * rows_dev * D,
        nbytes=4 << 20,
    )(stream, mix0, mix1, *returned)


def solution(mesh):
    return jax.shard_map(
        per_device,
        mesh=mesh,
        in_specs=(
            P("seq", "fsdp"),
            P("seq", "fsdp"),
            P(("seq", "fsdp"), None),
            P("fsdp", None),
            P(),
            P(),
            P(("seq", "fsdp"), None),
            P("seq", None, "fsdp"),
            P("seq", None, "fsdp"),
            P("seq", None, "fsdp"),
        ),
        out_specs=P(("seq", "fsdp"), None),
        check_vma=False,
    )
```

```python
import functools
import math

import jax
import jax.numpy as jnp
from jax import lax
from jax.experimental import pallas as pl
from jax.experimental.pallas import tpu as pltpu
from jax.sharding import PartitionSpec as P

D = 2880
HD = 64
WINDOW = 128
TOPK = 4
SLOTS = 8
EXPERTS = 64
CHUNKS = 2
PER = SLOTS // CHUNKS
F32 = jnp.float32
BF16 = jnp.bfloat16
NT = (((1,), (1,)), ((), ()))
TN = (((0,), (0,)), ((), ()))
VMEM = pl.BlockSpec(memory_space=pltpu.VMEM)
SMEM = pl.BlockSpec(memory_space=pltpu.SMEM)
ANY = pl.BlockSpec(memory_space=pl.ANY)


def call(body, outs, in_specs, scratch=(), limit=48):
    return pl.pallas_call(
        body,
        out_shape=outs,
        in_specs=in_specs,
        out_specs=jax.tree.map(lambda _: VMEM, outs),
        scratch_shapes=list(scratch),
        compiler_params=pltpu.CompilerParams(vmem_limit_bytes=limit << 20),
        cost_estimate=pl.CostEstimate(flops=1, bytes_accessed=1, transcendentals=0),
    )


def attention_body(place, q_ref, kv_ref, rim_ref, ow_ref, own_ref, to1, to2, to3, mixed):
    first, x = place[0] == 0, place[1]
    ext = jnp.concatenate([rim_ref[...], kv_ref[...]], axis=0)
    keys, values = ext[:, :HD], ext[:, HD:]
    row = lax.broadcasted_iota(jnp.int32, (WINDOW, 2 * WINDOW), 0)
    col = lax.broadcasted_iota(jnp.int32, (WINDOW, 2 * WINDOW), 1)
    band = (col >= row) & (col <= row + WINDOW)
    for b in range(2):
        allowed = band
        if b == 0:
            allowed = band & ((col >= WINDOW) | jnp.logical_not(first))
        k = keys[b * WINDOW : b * WINDOW + 2 * WINDOW]
        v = values[b * WINDOW : b * WINDOW + 2 * WINDOW]
        heads = []
        for h in range(q_ref.shape[1] // HD):
            q = q_ref[b * WINDOW : (b + 1) * WINDOW, h * HD : (h + 1) * HD]
            scores = lax.dot_general(q, k, NT, preferred_element_type=F32) * (1.0 / math.sqrt(HD))
            raised = jnp.where(allowed, jnp.exp(scores), 0.0)
            probs = (raised / jnp.sum(raised, axis=-1, keepdims=True)).astype(BF16)
            heads.append(jnp.dot(probs, v, preferred_element_type=F32))
        attended = jnp.concatenate(heads, axis=1).astype(BF16)
        for half in range(2):
            place_of = lax.rem(2 * b + half - x + 4, 4) * 64
            mixed[pl.ds(pl.multiple_of(place_of, 64), 64), :] = attended[half * 64 : half * 64 + 64]
    out = lax.dot_general(mixed[...], ow_ref[...], NT, preferred_element_type=F32)
    own_ref[...] = out[:64]
    to1[...] = out[64:128].astype(BF16)
    to2[...] = out[128:192].astype(BF16)
    to3[...] = out[192:].astype(BF16)


def norm_body(own, r1, r2, r3, hid, gain, pick0, pick1, stream_ref, normed_ref, out0, out1):
    projected = own[...] + r1[...].astype(F32) + r2[...].astype(F32) + r3[...].astype(F32)
    stream = (hid[...].astype(F32) + projected).astype(BF16)
    stream_ref[...] = stream
    wide = stream.astype(F32)
    inverse = lax.rsqrt(jnp.mean(wide * wide, axis=1, keepdims=True) + 1e-05)
    normed = (wide * inverse * gain[...]).astype(BF16)
    normed_ref[...] = normed
    for pick, out in ((pick0, out0), (pick1, out1)):
        rows = jnp.dot(pick[...], normed, preferred_element_type=F32)
        out[...] = rows.reshape(out.shape).astype(BF16)


def gates_body(normed, router, chosen_t, spread, pick0, pick1, mix0, mix1):
    logits = lax.dot_general(router[...], normed[...], NT, preferred_element_type=F32)
    raised = jnp.where(chosen_t[...] > 0.5, jnp.exp(logits), 0.0)
    gates = raised / jnp.sum(raised, axis=0, keepdims=True)
    rows = jnp.dot(spread[...], gates, preferred_element_type=F32, precision=lax.Precision.HIGHEST)
    for pick, mix in ((pick0, mix0), (pick1, mix1)):
        weight = pick[...].astype(F32) * rows
        high = weight.astype(BF16)
        low = (weight - high.astype(F32)).astype(BF16)
        mix[...] = jnp.concatenate([high, low], axis=1)


def flat(ref):
    return ref[...].reshape(ref.shape[0] * ref.shape[1], ref.shape[2])


def hidden_body(count, *refs):
    blocks, (gate, up), outs = refs[:count], refs[count : count + 2], refs[count + 2 : 2 * count + 2]
    vx, vw, sems = refs[2 * count + 2 :]
    width = gate.shape[1]
    weights = [
        pltpu.make_async_copy(gate, vw.at[:, :width], sems.at[0]),
        pltpu.make_async_copy(up, vw.at[:, width:], sems.at[1]),
    ]
    rows = [pltpu.make_async_copy(src, vx.at[i], sems.at[2 + i]) for i, src in enumerate(blocks)]
    for c in weights + rows:
        c.start()
    for c in weights:
        c.wait()
    for i in range(count):
        rows[i].wait()
        both = jnp.dot(flat(vx.at[i]), vw[...], preferred_element_type=F32)
        gate_vals, up_vals = both[:, :width], both[:, width:]
        act = gate_vals * jax.nn.sigmoid(1.702 * gate_vals) * (up_vals + 1.0)
        outs[i][...] = act.astype(BF16)


def down_body(*refs):
    hids, own, pieces = refs[:4], refs[4], refs[5:17]
    out, vw, acc, sems = refs[17:]
    long = pieces[0].shape[0]
    copies = [[pltpu.make_async_copy(own, vw.at[0], sems.at[0])]]
    for i in range(3):
        copies.append(
            [
                pltpu.make_async_copy(
                    pieces[4 * i + j], vw.at[1 + i, pl.ds(j * long, long)], sems.at[1 + 4 * i + j]
                )
                for j in range(4)
            ]
        )
    for group in copies:
        for c in group:
            c.start()
    for i in range(4):
        for c in copies[i]:
            c.wait()
        term = lax.dot_general(hids[i][...], vw[i], NT, preferred_element_type=F32)
        if i == 0:
            acc[...] = term
        elif i < 3:
            acc[...] += term
        else:
            out[...] = (acc[...] + term).reshape(out.shape).astype(BF16)


def combine_body(stream, mix0, mix1, ret0, ret1, out):
    both = lax.dot_general(mix0[...], flat(ret0), TN, preferred_element_type=F32)
    both += lax.dot_general(mix1[...], flat(ret1), TN, preferred_element_type=F32)
    out[...] = (stream[...].astype(F32) + both[:64] + both[64:]).astype(BF16)


def shape(*dims, dtype=BF16):
    return jax.ShapeDtypeStruct(dims, dtype)


def per_device(
    queries,
    keys_values,
    hidden_in,
    out_weight,
    norm_gain,
    router_weight,
    expert_ids,
    expert_gate,
    expert_up,
    expert_down,
):
    tok_dev = queries.shape[0]
    rows_dev = hidden_in.shape[0]
    gate, up, down = expert_gate[0], expert_up[0], expert_down[0]
    width = gate.shape[1]
    owners = lax.axis_size("seq")
    rows = owners * PER

    def shift(a, by):
        return lax.ppermute(a, "fsdp", [(i, (i + by) % 4) for i in range(4)])

    key_rim = lax.ppermute(
        keys_values[tok_dev - WINDOW :], "seq", [(i, i + 1) for i in range(owners - 1)]
    )
    long = D // 4
    pieces = [down[j * long : (j + 1) * long] for j in range(4)]
    left = [shift(p, 1) for p in pieces]
    right = [shift(p, -1) for p in pieces]
    far = [shift(left[0], 1), shift(left[1], 1), shift(right[2], -1), shift(right[3], -1)]

    chosen_t = jnp.any(
        expert_ids.T[:, None, :] == jnp.arange(EXPERTS, dtype=jnp.int32)[None, :, None], axis=0
    ).astype(F32)
    before = (jnp.arange(rows_dev)[:, None] < jnp.arange(rows_dev)[None, :]).astype(F32)
    rank_t = jnp.dot(chosen_t, before, preferred_element_type=F32)
    picks = []
    for c in range(CHUNKS):
        slot = (c * PER + jnp.arange(PER)).astype(F32)[None, :, None]
        hit = (chosen_t[:, None, :] > 0.5) & (rank_t[:, None, :] == slot)
        picks.append(hit.astype(BF16).reshape(rows, rows_dev))
    spread = (jnp.arange(rows)[:, None] // PER == jnp.arange(EXPERTS)[None, :]).astype(F32)

    place = jnp.stack([lax.axis_index("seq"), lax.axis_index("fsdp")]).astype(jnp.int32)
    own, to1, to2, to3 = call(
        attention_body,
        (shape(rows_dev, D, dtype=F32),) + (shape(rows_dev, D),) * 3,
        [SMEM] + [VMEM] * 4,
        [pltpu.VMEM((tok_dev, queries.shape[1]), BF16)],
    )(place, queries, keys_values, key_rim, out_weight.T)
    r1, r2, r3 = shift(to1, 1), shift(to2, 2), shift(to3, 3)
    own, left[0], right[3] = lax.optimization_barrier((own, left[0], right[3]))
    stream, normed, out0, out1 = call(
        norm_body,
        (shape(rows_dev, D),) * 2 + (shape(owners, PER, D),) * 2,
        [VMEM] * 8,
    )(own, r1, r2, r3, hidden_in, norm_gain[None, :], *picks)

    def exchange(a):
        return lax.all_to_all(a, "seq", split_axis=0, concat_axis=0, tiled=True)

    received = [exchange(out0)]
    out1, left[1:], right[:3], far[0], far[3] = lax.optimization_barrier(
        (out1, left[1:], right[:3], far[0], far[3])
    )
    received.append(exchange(out1))
    mix0, mix1 = call(
        gates_body,
        (shape(rows, 2 * rows_dev),) * 2,
        [VMEM] * 6,
    )(normed, router_weight.T, chosen_t, spread, *picks)

    def hidden(*blocks):
        count = len(blocks)
        return call(
            functools.partial(hidden_body, count),
            (shape(rows, width),) * count,
            [ANY] * (count + 2),
            [
                pltpu.VMEM((count, owners, PER, D), BF16),
                pltpu.VMEM((D, 2 * width), BF16),
                pltpu.SemaphoreType.DMA((count + 2,)),
            ],
        )(*blocks, gate, up)

    def around(mine):
        return shift(mine, 1), shift(mine, -1)

    def opposite(from_left, from_right):
        half = owners // 2
        return jnp.concatenate(
            [shift(from_left[:half], 1), shift(from_right[half:], -1)], axis=0
        )

    def answer(hid_own, hid_left, hid_right, hid_far):
        return call(
            down_body,
            shape(owners, PER, D),
            [VMEM] * 4 + [ANY] * 13,
            [
                pltpu.VMEM((4, D, width), BF16),
                pltpu.VMEM((rows, D), F32),
                pltpu.SemaphoreType.DMA((13,)),
            ],
        )(
            hid_own, shift(hid_right, 1), shift(hid_left, -1), shift(hid_far, 2),
            down, *left, *right, *far,
        )

    first, second = received
    beside, far[1], far[2] = lax.optimization_barrier((around(first), far[1], far[2]))
    hids = hidden(first, *beside)
    last, second, hids = lax.optimization_barrier((opposite(*beside), second, hids))
    answer0 = answer(*hids, *hidden(last))
    answer0, beside = lax.optimization_barrier((answer0, around(second)))
    returned = [exchange(answer0)]
    hids = hidden(second, *beside)
    returned.append(exchange(answer(*hids, *hidden(opposite(*beside)))))
    return call(
        combine_body,
        shape(rows_dev, D),
        [VMEM] * 5,
    )(stream, mix0, mix1, *returned)


def solution(mesh):
    return jax.shard_map(
        per_device,
        mesh=mesh,
        in_specs=(
            P("seq", "fsdp"),
            P("seq", "fsdp"),
            P(("seq", "fsdp"), None),
            P("fsdp", None),
            P(),
            P(),
            P(("seq", "fsdp"), None),
            P("seq", None, "fsdp"),
            P("seq", None, "fsdp"),
            P("seq", None, "fsdp"),
        ),
        out_specs=P(("seq", "fsdp"), None),
        check_vma=False,
    )
```

```python
import functools
import math

import jax
import jax.numpy as jnp
from jax import lax
from jax.experimental import pallas as pl
from jax.experimental.pallas import tpu as pltpu
from jax.sharding import PartitionSpec as P

D = 2880
HD = 64
WINDOW = 128
TOPK = 4
SLOTS = 8
EXPERTS = 64
CHUNKS = 2
PER = SLOTS // CHUNKS
F32 = jnp.float32
BF16 = jnp.bfloat16
NT = (((1,), (1,)), ((), ()))
TN = (((0,), (0,)), ((), ()))
VMEM = pl.BlockSpec(memory_space=pltpu.VMEM)
ANY = pl.BlockSpec(memory_space=pl.ANY)
SMEM = pl.BlockSpec(memory_space=pltpu.SMEM)


def call(body, outs, in_specs, scratch=(), limit=20):
    return pl.pallas_call(
        body,
        out_shape=outs,
        in_specs=in_specs,
        out_specs=jax.tree.map(lambda _: VMEM, outs),
        scratch_shapes=list(scratch),
        compiler_params=pltpu.CompilerParams(vmem_limit_bytes=limit << 20),
        cost_estimate=pl.CostEstimate(flops=1, bytes_accessed=1, transcendentals=0),
    )


def attention_body(place, q_ref, kv_ref, rim_ref, ow_ref, own_ref, to1, to2, to3, mixed):
    first, x = place[0] == 0, place[1]
    ext = jnp.concatenate([rim_ref[...], kv_ref[...]], axis=0)
    keys, values = ext[:, :HD], ext[:, HD:]
    row = lax.broadcasted_iota(jnp.int32, (WINDOW, 2 * WINDOW), 0)
    col = lax.broadcasted_iota(jnp.int32, (WINDOW, 2 * WINDOW), 1)
    band = (col >= row) & (col <= row + WINDOW)
    for b in range(2):
        allowed = band
        if b == 0:
            allowed = band & ((col >= WINDOW) | jnp.logical_not(first))
        k = keys[b * WINDOW : b * WINDOW + 2 * WINDOW]
        v = values[b * WINDOW : b * WINDOW + 2 * WINDOW]
        heads = []
        for h in range(q_ref.shape[1] // HD):
            q = q_ref[b * WINDOW : (b + 1) * WINDOW, h * HD : (h + 1) * HD]
            scores = lax.dot_general(q, k, NT, preferred_element_type=F32) * (1.0 / math.sqrt(HD))
            raised = jnp.where(allowed, jnp.exp(scores), 0.0)
            probs = (raised / jnp.sum(raised, axis=-1, keepdims=True)).astype(BF16)
            heads.append(jnp.dot(probs, v, preferred_element_type=F32))
        attended = jnp.concatenate(heads, axis=1).astype(BF16)
        for half in range(2):
            place_of = lax.rem(2 * b + half - x + 4, 4) * 64
            mixed[pl.ds(pl.multiple_of(place_of, 64), 64), :] = attended[half * 64 : half * 64 + 64]
    out = lax.dot_general(mixed[...], ow_ref[...], NT, preferred_element_type=F32)
    own_ref[...] = out[:64]
    to1[...] = out[64:128].astype(BF16)
    to2[...] = out[128:192].astype(BF16)
    to3[...] = out[192:].astype(BF16)


def norm_body(own, r1, r2, r3, hid, gain, pick0, pick1, stream_ref, normed_ref, out0, out1):
    projected = own[...] + r1[...].astype(F32) + r2[...].astype(F32) + r3[...].astype(F32)
    stream = (hid[...].astype(F32) + projected).astype(BF16)
    stream_ref[...] = stream
    wide = stream.astype(F32)
    inverse = lax.rsqrt(jnp.mean(wide * wide, axis=1, keepdims=True) + 1e-05)
    normed = (wide * inverse * gain[...]).astype(BF16)
    normed_ref[...] = normed
    for pick, out in ((pick0, out0), (pick1, out1)):
        rows = jnp.dot(pick[...], normed, preferred_element_type=F32)
        out[...] = rows.reshape(out.shape).astype(BF16)


def cell(rows, by):
    row = lax.broadcasted_iota(jnp.int32, (rows, EXPERTS), 0)
    expert = lax.broadcasted_iota(jnp.int32, (rows, EXPERTS), 1)
    return row - expert * PER == by


def routing_body(ids, chosen_ref, *picks):
    tokens = ids.shape[1]
    expert = lax.broadcasted_iota(jnp.int32, (EXPERTS, tokens), 0)
    chosen = expert == ids[0:1]
    for k in range(1, TOPK):
        chosen |= expert == ids[k : k + 1]
    chosen = chosen.astype(F32)
    chosen_ref[...] = chosen
    earlier = lax.broadcasted_iota(jnp.int32, (tokens, tokens), 0)
    later = lax.broadcasted_iota(jnp.int32, (tokens, tokens), 1)
    rank = jnp.dot(
        chosen.astype(BF16), (earlier < later).astype(BF16), preferred_element_type=F32
    )
    for c, pick in enumerate(picks):
        total = jnp.zeros(pick.shape, F32)
        for by in range(PER):
            hit = jnp.where(rank == float(c * PER + by), chosen, 0.0).astype(BF16)
            total += jnp.dot(
                cell(pick.shape[0], by).astype(BF16), hit, preferred_element_type=F32
            )
        pick[...] = total.astype(BF16)


def gates_body(normed, router, chosen, pick0, pick1, mix0, mix1):
    logits = lax.dot_general(router[...], normed[...], NT, preferred_element_type=F32)
    raised = jnp.where(chosen[...] > 0.5, jnp.exp(logits), 0.0)
    gates = raised / jnp.sum(raised, axis=0, keepdims=True)
    rows = pick0.shape[0]
    spread = cell(rows, 0)
    for by in range(1, PER):
        spread |= cell(rows, by)
    spread = spread.astype(F32)
    gates = jnp.dot(spread, gates, preferred_element_type=F32, precision=lax.Precision.HIGHEST)
    for pick, mix in ((pick0, mix0), (pick1, mix1)):
        weight = pick[...].astype(F32) * gates
        high = weight.astype(BF16)
        low = (weight - high.astype(F32)).astype(BF16)
        mix[...] = jnp.concatenate([high, low], axis=1)


def flat(ref):
    return ref[...].reshape(ref.shape[0] * ref.shape[1], ref.shape[2])


def activated(rows, both):
    vals = jnp.dot(rows, both[...], preferred_element_type=F32)
    gate, up = jnp.split(vals, 2, axis=1)
    return (gate * jax.nn.sigmoid(1.702 * gate) * (up + 1.0)).astype(BF16)


def hidden_body(parts, *refs):
    count = len(parts)
    blocks, both, outs = refs[: sum(parts)], refs[sum(parts)], refs[-count:]
    at = 0
    for n, out in zip(parts, outs, strict=True):
        rows = flat(blocks[at])
        if n == 2:
            rows = jnp.concatenate([rows, flat(blocks[at + 1])], axis=0)
        at += n
        out[...] = activated(rows, both)


def hidden_all_body(place, blocks, both, *refs):
    outs, (vx, sems) = refs[:4], refs[4:]
    owners = vx.shape[1]
    order = (2, 1, 3, 0)
    copies = [
        pltpu.make_async_copy(
            blocks.at[pl.ds(lax.rem(place[1] + by, 4) * owners, owners)], vx.at[by], sems.at[by]
        )
        for by in range(4)
    ]
    for by in order:
        copies[by].start()
    for by in order:
        copies[by].wait()
        rows = flat(vx.at[by])
        outs[by][...] = activated(rows, both)


BANDS = [(0, 640), (640, 640), (1280, 640), (1920, 640), (2560, 320)]


def down_body(place, h0, h1, h2, h3, shards, out):
    for at, long in BANDS:
        total = None
        for by, hid in enumerate((h0, h1, h2, h3)):
            shard = shards[lax.rem(place[1] + by, 4), at : at + long, :]
            term = lax.dot_general(hid[...], shard, NT, preferred_element_type=F32)
            total = term if by == 0 else total + term
        out[:, :, at : at + long] = total.reshape(out.shape[0], out.shape[1], long).astype(BF16)


def combine_body(stream, mix0, mix1, ret0, ret1, out):
    both = lax.dot_general(mix0[...], flat(ret0), TN, preferred_element_type=F32)
    both += lax.dot_general(mix1[...], flat(ret1), TN, preferred_element_type=F32)
    out[...] = (stream[...].astype(F32) + both[:64] + both[64:]).astype(BF16)


def shape(*dims, dtype=BF16):
    return jax.ShapeDtypeStruct(dims, dtype)


def per_device(
    queries,
    keys_values,
    hidden_in,
    out_weight,
    norm_gain,
    router_weight,
    expert_ids,
    expert_gate,
    expert_up,
    expert_down,
):
    tok_dev = queries.shape[0]
    rows_dev = hidden_in.shape[0]
    gate, up, down = expert_gate[0], expert_up[0], expert_down[0]
    width = gate.shape[1]
    owners = lax.axis_size("seq")
    rows = owners * PER

    def shift(a, by):
        return lax.ppermute(a, "fsdp", [(i, (i + by) % 4) for i in range(4)])

    key_rim = lax.ppermute(
        keys_values[tok_dev - WINDOW :], "seq", [(i, i + 1) for i in range(owners - 1)]
    )
    downs = lax.all_gather(down, "fsdp", axis=0)

    place = jnp.stack([lax.axis_index("seq"), lax.axis_index("fsdp")]).astype(jnp.int32)
    own, to1, to2, to3 = call(
        attention_body,
        (shape(rows_dev, D, dtype=F32),) + (shape(rows_dev, D),) * 3,
        [SMEM] + [VMEM] * 4,
        [pltpu.VMEM((tok_dev, queries.shape[1]), BF16)],
    )(place, queries, keys_values, key_rim, out_weight.T)
    r1, r2, r3 = shift(to1, 1), shift(to2, 2), shift(to3, 3)

    expert_ids, own = lax.optimization_barrier((expert_ids, own))
    chosen, *picks = call(
        routing_body,
        (shape(EXPERTS, rows_dev, dtype=F32),) + (shape(rows, rows_dev),) * CHUNKS,
        [VMEM],
    )(expert_ids.T)

    stream, normed, out0, out1 = call(
        norm_body,
        (shape(rows_dev, D),) * 2 + (shape(owners, PER, D),) * 2,
        [VMEM] * 8,
    )(own, r1, r2, r3, hidden_in, norm_gain[None, :], *picks)

    def exchange(a):
        return lax.all_to_all(a, "seq", split_axis=0, concat_axis=0, tiled=True)

    first = exchange(out0)
    out1, first = lax.optimization_barrier((out1, first))
    second = exchange(out1)
    mix0, mix1 = call(
        gates_body,
        (shape(rows, 2 * rows_dev),) * 2,
        [VMEM] * 5,
    )(normed, router_weight.T, chosen, *picks)

    half = owners // 2
    both = jnp.concatenate([gate, up], axis=1)

    def hidden(parts, *blocks):
        return call(
            functools.partial(hidden_body, parts),
            (shape(rows, width),) * len(parts),
            [VMEM] * (sum(parts) + 1),
        )(*blocks, both)

    def around(mine):
        low, high = mine[:half], mine[half:]
        return shift(low, 1), shift(high, -1), shift(high, 1), shift(low, -1)

    def near(mine, left_low, right_high, left_high, right_low):
        return hidden((1, 2, 2), mine, left_low, left_high, right_low, right_high)

    def opposite(left_low, right_high):
        return shift(left_low, 1), shift(right_high, -1)

    def back(hid_left, hid_right):
        return shift(hid_right, 1), shift(hid_left, -1)

    def answer(hid_own, from_left, from_right, from_far):
        return call(
            down_body,
            shape(owners, PER, D),
            [SMEM] + [VMEM] * 5,
        )(place, hid_own, from_right, from_far, from_left, downs)

    beside = around(first)
    halves = opposite(*beside[:2])
    beside, second, downs = lax.optimization_barrier((beside, second, downs))
    everyone = lax.all_gather(second, "fsdp", axis=0, tiled=True)
    own0, left0, right0 = near(first, *beside)
    halves, left0, right0 = lax.optimization_barrier((halves, left0, right0))
    (far0,) = hidden((2,), *halves)
    answer0 = answer(own0, *back(left0, right0), shift(far0, 2))
    returned = [exchange(answer0)]
    both, _ = lax.optimization_barrier((both, answer0))
    hids = call(
        hidden_all_body,
        (shape(rows, width),) * 4,
        [SMEM, ANY, VMEM],
        [pltpu.VMEM((4, owners, PER, D), BF16), pltpu.SemaphoreType.DMA((4,))],
    )(place, everyone, both)
    own1, far1 = hids[0], shift(hids[2], 2)
    returned.append(exchange(answer(own1, *back(hids[3], hids[1]), far1)))
    return call(
        combine_body,
        shape(rows_dev, D),
        [VMEM] * 5,
    )(stream, mix0, mix1, *returned)


def solution(mesh):
    return jax.shard_map(
        per_device,
        mesh=mesh,
        in_specs=(
            P("seq", "fsdp"),
            P("seq", "fsdp"),
            P(("seq", "fsdp"), None),
            P("fsdp", None),
            P(),
            P(),
            P(("seq", "fsdp"), None),
            P("seq", None, "fsdp"),
            P("seq", None, "fsdp"),
            P("seq", None, "fsdp"),
        ),
        out_specs=P(("seq", "fsdp"), None),
        check_vma=False,
    )
```

```python
import functools
import math

import jax
import jax.numpy as jnp
from jax import lax
from jax.experimental import pallas as pl
from jax.experimental.pallas import tpu as pltpu
from jax.sharding import PartitionSpec as P

D = 2880
HD = 64
WINDOW = 128
TOPK = 4
SLOTS = 8
EXPERTS = 64
CHUNKS = 2
PER = SLOTS // CHUNKS
F32 = jnp.float32
BF16 = jnp.bfloat16
NT = (((1,), (1,)), ((), ()))
TN = (((0,), (0,)), ((), ()))
VMEM = pl.BlockSpec(memory_space=pltpu.VMEM)
ANY = pl.BlockSpec(memory_space=pl.ANY)
SMEM = pl.BlockSpec(memory_space=pltpu.SMEM)


def call(body, outs, in_specs, scratch=(), limit=24):
    return pl.pallas_call(
        body,
        out_shape=outs,
        in_specs=in_specs,
        out_specs=jax.tree.map(lambda _: VMEM, outs),
        scratch_shapes=list(scratch),
        compiler_params=pltpu.CompilerParams(vmem_limit_bytes=limit << 20),
        cost_estimate=pl.CostEstimate(flops=1, bytes_accessed=1, transcendentals=0),
    )


def attention_body(place, q_ref, kv_ref, rim_ref, ow_ref, own_ref, to1, to2, to3, mixed):
    first, x = place[0] == 0, place[1]
    ext = jnp.concatenate([rim_ref[...], kv_ref[...]], axis=0)
    keys, values = ext[:, :HD], ext[:, HD:]
    row = lax.broadcasted_iota(jnp.int32, (WINDOW, 2 * WINDOW), 0)
    col = lax.broadcasted_iota(jnp.int32, (WINDOW, 2 * WINDOW), 1)
    band = (col >= row) & (col <= row + WINDOW)
    for b in range(2):
        allowed = band
        if b == 0:
            allowed = band & ((col >= WINDOW) | jnp.logical_not(first))
        k = keys[b * WINDOW : b * WINDOW + 2 * WINDOW]
        v = values[b * WINDOW : b * WINDOW + 2 * WINDOW]
        heads = []
        for h in range(q_ref.shape[1] // HD):
            q = q_ref[b * WINDOW : (b + 1) * WINDOW, h * HD : (h + 1) * HD]
            scores = lax.dot_general(q, k, NT, preferred_element_type=F32) * (1.0 / math.sqrt(HD))
            raised = jnp.where(allowed, jnp.exp(scores), 0.0)
            probs = (raised / jnp.sum(raised, axis=-1, keepdims=True)).astype(BF16)
            heads.append(jnp.dot(probs, v, preferred_element_type=F32))
        attended = jnp.concatenate(heads, axis=1).astype(BF16)
        for half in range(2):
            place_of = lax.rem(2 * b + half - x + 4, 4) * 64
            mixed[pl.ds(pl.multiple_of(place_of, 64), 64), :] = attended[half * 64 : half * 64 + 64]
    out = lax.dot_general(mixed[...], ow_ref[...], NT, preferred_element_type=F32)
    own_ref[...] = out[:64]
    to1[...] = out[64:128].astype(BF16)
    to2[...] = out[128:192].astype(BF16)
    to3[...] = out[192:].astype(BF16)


def norm_body(own, r1, r2, r3, hid, gain, pick0, pick1, stream_ref, normed_ref, out0, out1):
    projected = own[...] + r1[...].astype(F32) + r2[...].astype(F32) + r3[...].astype(F32)
    stream = (hid[...].astype(F32) + projected).astype(BF16)
    stream_ref[...] = stream
    wide = stream.astype(F32)
    inverse = lax.rsqrt(jnp.mean(wide * wide, axis=1, keepdims=True) + 1e-05)
    normed = (wide * inverse * gain[...]).astype(BF16)
    normed_ref[...] = normed
    for pick, out in ((pick0, out0), (pick1, out1)):
        rows = jnp.dot(pick[...], normed, preferred_element_type=F32)
        out[...] = rows.reshape(out.shape).astype(BF16)


def cell(rows, by):
    row = lax.broadcasted_iota(jnp.int32, (rows, EXPERTS), 0)
    expert = lax.broadcasted_iota(jnp.int32, (rows, EXPERTS), 1)
    return row - expert * PER == by


def routing_body(ids, chosen_ref, *picks):
    tokens = ids.shape[1]
    expert = lax.broadcasted_iota(jnp.int32, (EXPERTS, tokens), 0)
    chosen = expert == ids[0:1]
    for k in range(1, TOPK):
        chosen |= expert == ids[k : k + 1]
    chosen = chosen.astype(F32)
    chosen_ref[...] = chosen
    earlier = lax.broadcasted_iota(jnp.int32, (tokens, tokens), 0)
    later = lax.broadcasted_iota(jnp.int32, (tokens, tokens), 1)
    rank = jnp.dot(
        chosen.astype(BF16), (earlier < later).astype(BF16), preferred_element_type=F32
    )
    for c, pick in enumerate(picks):
        total = jnp.zeros(pick.shape, F32)
        for by in range(PER):
            hit = jnp.where(rank == float(c * PER + by), chosen, 0.0).astype(BF16)
            total += jnp.dot(
                cell(pick.shape[0], by).astype(BF16), hit, preferred_element_type=F32
            )
        pick[...] = total.astype(BF16)


def gates_body(normed, router, chosen, pick0, pick1, mix0, mix1):
    logits = lax.dot_general(router[...], normed[...], NT, preferred_element_type=F32)
    raised = jnp.where(chosen[...] > 0.5, jnp.exp(logits), 0.0)
    gates = raised / jnp.sum(raised, axis=0, keepdims=True)
    rows = pick0.shape[0]
    spread = cell(rows, 0)
    for by in range(1, PER):
        spread |= cell(rows, by)
    spread = spread.astype(F32)
    gates = jnp.dot(spread, gates, preferred_element_type=F32, precision=lax.Precision.HIGHEST)
    for pick, mix in ((pick0, mix0), (pick1, mix1)):
        weight = pick[...].astype(F32) * gates
        high = weight.astype(BF16)
        low = (weight - high.astype(F32)).astype(BF16)
        mix[...] = jnp.concatenate([high, low], axis=1)


def flat(ref):
    return ref[...].reshape(ref.shape[0] * ref.shape[1], ref.shape[2])


SPLIT = 1536


def hidden_body(parts, *refs):
    count, given = len(parts), sum(parts)
    blocks, both, outs = refs[:given], refs[given], refs[given + 1 : given + 1 + count]
    vx, vw, sems = refs[given + 1 + count :]
    spans = (pl.ds(0, SPLIT), pl.ds(SPLIT, both.shape[0] - SPLIT))
    weights = [
        pltpu.make_async_copy(both.at[span], vw.at[span], sems.at[n])
        for n, span in enumerate(spans)
    ]
    rows, n = [], 0
    for i, many in enumerate(parts):
        long = vx.shape[1] // many
        rows.append(
            [
                pltpu.make_async_copy(
                    blocks[n + j], vx.at[i, pl.ds(j * long, long)], sems.at[2 + n + j]
                )
                for j in range(many)
            ]
        )
        n += many
    for c in (*rows[0], *weights, *(c for group in rows[1:] for c in group)):
        c.start()
    for i, group in enumerate(rows):
        for c in group:
            c.wait()
        block = flat(vx.at[i])
        vals = None
        for span, c in zip(spans, weights, strict=True):
            if i == 0:
                c.wait()
            at, long = span.start, span.size
            term = jnp.dot(
                block[:, at : at + long], vw[at : at + long], preferred_element_type=F32
            )
            vals = term if vals is None else vals + term
        gate, up = jnp.split(vals, 2, axis=1)
        outs[i][...] = (gate * jax.nn.sigmoid(1.702 * gate) * (up + 1.0)).astype(BF16)


BANDS = [(0, 640), (640, 640), (1280, 640), (1920, 640), (2560, 320)]


def down_body(place, h0, h1, h2, h3, shards, out):
    for at, long in BANDS:
        total = None
        for by, hid in enumerate((h0, h1, h2, h3)):
            shard = shards[lax.rem(place[1] + by, 4), at : at + long, :]
            term = lax.dot_general(hid[...], shard, NT, preferred_element_type=F32)
            total = term if by == 0 else total + term
        out[:, :, at : at + long] = total.reshape(out.shape[0], out.shape[1], long).astype(BF16)


def combine_body(stream, mix0, mix1, ret0, ret1, out):
    both = lax.dot_general(mix0[...], flat(ret0), TN, preferred_element_type=F32)
    both += lax.dot_general(mix1[...], flat(ret1), TN, preferred_element_type=F32)
    out[...] = (stream[...].astype(F32) + both[:64] + both[64:]).astype(BF16)


def shape(*dims, dtype=BF16):
    return jax.ShapeDtypeStruct(dims, dtype)


def per_device(
    queries,
    keys_values,
    hidden_in,
    out_weight,
    norm_gain,
    router_weight,
    expert_ids,
    expert_gate,
    expert_up,
    expert_down,
):
    tok_dev = queries.shape[0]
    rows_dev = hidden_in.shape[0]
    gate, up, down = expert_gate[0], expert_up[0], expert_down[0]
    width = gate.shape[1]
    owners = lax.axis_size("seq")
    rows = owners * PER

    def shift(a, by):
        return lax.ppermute(a, "fsdp", [(i, (i + by) % 4) for i in range(4)])

    downs = lax.all_gather(down, "fsdp", axis=0)
    key_rim = lax.ppermute(
        keys_values[tok_dev - WINDOW :], "seq", [(i, i + 1) for i in range(owners - 1)]
    )

    place = jnp.stack([lax.axis_index("seq"), lax.axis_index("fsdp")]).astype(jnp.int32)
    own, to1, to2, to3 = call(
        attention_body,
        (shape(rows_dev, D, dtype=F32),) + (shape(rows_dev, D),) * 3,
        [SMEM] + [VMEM] * 4,
        [pltpu.VMEM((tok_dev, queries.shape[1]), BF16)],
    )(place, queries, keys_values, key_rim, out_weight.T)
    r1, r2, r3 = shift(to1, 1), shift(to2, 2), shift(to3, 3)

    expert_ids, own = lax.optimization_barrier((expert_ids, own))
    chosen, *picks = call(
        routing_body,
        (shape(EXPERTS, rows_dev, dtype=F32),) + (shape(rows, rows_dev),) * CHUNKS,
        [VMEM],
    )(expert_ids.T)

    stream, normed, out0, out1 = call(
        norm_body,
        (shape(rows_dev, D),) * 2 + (shape(owners, PER, D),) * 2,
        [VMEM] * 8,
    )(own, r1, r2, r3, hidden_in, norm_gain[None, :], *picks)

    def exchange(a):
        return lax.all_to_all(a, "seq", split_axis=0, concat_axis=0, tiled=True)

    first = exchange(out0)
    out1, first = lax.optimization_barrier((out1, first))
    second = exchange(out1)
    mix0, mix1 = call(
        gates_body,
        (shape(rows, 2 * rows_dev),) * 2,
        [VMEM] * 5,
    )(normed, router_weight.T, chosen, *picks)

    half = owners // 2
    both = jnp.concatenate([gate, up], axis=1)

    def hidden(parts, *blocks):
        return call(
            functools.partial(hidden_body, parts),
            (shape(rows, width),) * len(parts),
            [ANY] * (sum(parts) + 1),
            [
                pltpu.VMEM((len(parts), owners, PER, D), BF16),
                pltpu.VMEM((D, 2 * width), BF16),
                pltpu.SemaphoreType.DMA((sum(parts) + 2,)),
            ],
        )(*blocks, both)

    def around(mine):
        low, high = mine[:half], mine[half:]
        return shift(low, 1), shift(high, -1), shift(high, 1), shift(low, -1)

    def near(mine, left_low, right_high, left_high, right_low):
        return hidden((1, 2, 2), mine, left_low, left_high, right_low, right_high)

    def opposite(left_low, right_high):
        return shift(left_low, 1), shift(right_high, -1)

    def back(hid_left, hid_right):
        return shift(hid_right, 1), shift(hid_left, -1)

    def answer(hid_own, from_left, from_right, from_far):
        return call(
            down_body,
            shape(owners, PER, D),
            [SMEM] + [VMEM] * 5,
        )(place, hid_own, from_right, from_far, from_left, downs)

    beside = around(first)
    halves = opposite(*beside[:2])
    beside, downs, second = lax.optimization_barrier((beside, downs, second))
    low, high = second[:half], second[half:]
    own0, left0, right0 = near(first, *beside)
    halves, left0, right0 = lax.optimization_barrier((halves, left0, right0))
    (far0,) = hidden((2,), *halves)
    ready = shift(low, 1), shift(high, -1)
    moved = (*back(left0, right0), shift(far0, 2))
    low, high, moved, ready = lax.optimization_barrier((low, high, moved, ready))
    later = shift(high, 1), shift(low, -1)
    answer0 = answer(own0, *moved)
    answer0, ready, later = lax.optimization_barrier((answer0, ready, later))
    returned = [exchange(answer0)]
    own1, left1, right1 = near(second, *ready, *later)
    (far1,) = hidden((2,), *opposite(*ready))
    returned.append(exchange(answer(own1, *back(left1, right1), shift(far1, 2))))
    return call(
        combine_body,
        shape(rows_dev, D),
        [VMEM] * 5,
    )(stream, mix0, mix1, *returned)


def solution(mesh):
    return jax.shard_map(
        per_device,
        mesh=mesh,
        in_specs=(
            P("seq", "fsdp"),
            P("seq", "fsdp"),
            P(("seq", "fsdp"), None),
            P("fsdp", None),
            P(),
            P(),
            P(("seq", "fsdp"), None),
            P("seq", None, "fsdp"),
            P("seq", None, "fsdp"),
            P("seq", None, "fsdp"),
        ),
        out_specs=P(("seq", "fsdp"), None),
        check_vma=False,
    )
```

```python
import functools
import math

import jax
import jax.numpy as jnp
from jax import lax
from jax.experimental import pallas as pl
from jax.experimental.pallas import tpu as pltpu
from jax.sharding import PartitionSpec as P

D = 2880
HD = 64
WINDOW = 128
TOPK = 4
SLOTS = 8
EXPERTS = 64
CHUNKS = 2
PER = SLOTS // CHUNKS
F32 = jnp.float32
BF16 = jnp.bfloat16
NT = (((1,), (1,)), ((), ()))
TN = (((0,), (0,)), ((), ()))
VMEM = pl.BlockSpec(memory_space=pltpu.VMEM)
ANY = pl.BlockSpec(memory_space=pl.ANY)
SMEM = pl.BlockSpec(memory_space=pltpu.SMEM)


def call(body, outs, in_specs, scratch=(), limit=24):
    return pl.pallas_call(
        body,
        out_shape=outs,
        in_specs=in_specs,
        out_specs=jax.tree.map(lambda _: VMEM, outs),
        scratch_shapes=list(scratch),
        compiler_params=pltpu.CompilerParams(vmem_limit_bytes=limit << 20),
        cost_estimate=pl.CostEstimate(flops=1, bytes_accessed=1, transcendentals=0),
    )


def attention_body(place, q_ref, kv_ref, rim_ref, ow_ref, own_ref, to1, to2, to3, mixed):
    first, x = place[0] == 0, place[1]
    ext = jnp.concatenate([rim_ref[...], kv_ref[...]], axis=0)
    keys, values = ext[:, :HD], ext[:, HD:]
    row = lax.broadcasted_iota(jnp.int32, (WINDOW, 2 * WINDOW), 0)
    col = lax.broadcasted_iota(jnp.int32, (WINDOW, 2 * WINDOW), 1)
    band = (col >= row) & (col <= row + WINDOW)
    for b in range(2):
        allowed = band
        if b == 0:
            allowed = band & ((col >= WINDOW) | jnp.logical_not(first))
        k = keys[b * WINDOW : b * WINDOW + 2 * WINDOW]
        v = values[b * WINDOW : b * WINDOW + 2 * WINDOW]
        heads = []
        for h in range(q_ref.shape[1] // HD):
            q = q_ref[b * WINDOW : (b + 1) * WINDOW, h * HD : (h + 1) * HD]
            scores = lax.dot_general(q, k, NT, preferred_element_type=F32) * (1.0 / math.sqrt(HD))
            raised = jnp.where(allowed, jnp.exp(scores), 0.0)
            probs = (raised / jnp.sum(raised, axis=-1, keepdims=True)).astype(BF16)
            heads.append(jnp.dot(probs, v, preferred_element_type=F32))
        attended = jnp.concatenate(heads, axis=1).astype(BF16)
        for half in range(2):
            place_of = lax.rem(2 * b + half - x + 4, 4) * 64
            mixed[pl.ds(pl.multiple_of(place_of, 64), 64), :] = attended[half * 64 : half * 64 + 64]
    out = lax.dot_general(mixed[...], ow_ref[...], NT, preferred_element_type=F32)
    own_ref[...] = out[:64]
    to1[...] = out[64:128].astype(BF16)
    to2[...] = out[128:192].astype(BF16)
    to3[...] = out[192:].astype(BF16)


def norm_body(own, r1, r2, r3, hid, gain, pick0, pick1, stream_ref, normed_ref, out0, out1):
    projected = own[...] + r1[...].astype(F32) + r2[...].astype(F32) + r3[...].astype(F32)
    stream = (hid[...].astype(F32) + projected).astype(BF16)
    stream_ref[...] = stream
    wide = stream.astype(F32)
    inverse = lax.rsqrt(jnp.mean(wide * wide, axis=1, keepdims=True) + 1e-05)
    normed = (wide * inverse * gain[...]).astype(BF16)
    normed_ref[...] = normed
    for pick, out in ((pick0, out0), (pick1, out1)):
        rows = jnp.dot(pick[...], normed, preferred_element_type=F32)
        out[...] = rows.reshape(out.shape).astype(BF16)


def cell(rows, by):
    row = lax.broadcasted_iota(jnp.int32, (rows, EXPERTS), 0)
    expert = lax.broadcasted_iota(jnp.int32, (rows, EXPERTS), 1)
    return row - expert * PER == by


def routing_body(ids, chosen_ref, *picks):
    tokens = ids.shape[1]
    expert = lax.broadcasted_iota(jnp.int32, (EXPERTS, tokens), 0)
    chosen = expert == ids[0:1]
    for k in range(1, TOPK):
        chosen |= expert == ids[k : k + 1]
    chosen = chosen.astype(F32)
    chosen_ref[...] = chosen
    earlier = lax.broadcasted_iota(jnp.int32, (tokens, tokens), 0)
    later = lax.broadcasted_iota(jnp.int32, (tokens, tokens), 1)
    rank = jnp.dot(
        chosen.astype(BF16), (earlier < later).astype(BF16), preferred_element_type=F32
    )
    for c, pick in enumerate(picks):
        total = jnp.zeros(pick.shape, F32)
        for by in range(PER):
            hit = jnp.where(rank == float(c * PER + by), chosen, 0.0).astype(BF16)
            total += jnp.dot(
                cell(pick.shape[0], by).astype(BF16), hit, preferred_element_type=F32
            )
        pick[...] = total.astype(BF16)


def gates_body(normed, router, chosen, pick0, pick1, mix0, mix1):
    logits = lax.dot_general(router[...], normed[...], NT, preferred_element_type=F32)
    raised = jnp.where(chosen[...] > 0.5, jnp.exp(logits), 0.0)
    gates = raised / jnp.sum(raised, axis=0, keepdims=True)
    rows = pick0.shape[0]
    spread = cell(rows, 0)
    for by in range(1, PER):
        spread |= cell(rows, by)
    spread = spread.astype(F32)
    gates = jnp.dot(spread, gates, preferred_element_type=F32, precision=lax.Precision.HIGHEST)
    for pick, mix in ((pick0, mix0), (pick1, mix1)):
        weight = pick[...].astype(F32) * gates
        high = weight.astype(BF16)
        low = (weight - high.astype(F32)).astype(BF16)
        mix[...] = jnp.concatenate([high, low], axis=1)


def flat(ref):
    return ref[...].reshape(ref.shape[0] * ref.shape[1], ref.shape[2])


SPLIT = 1536


def hidden_body(parts, *refs):
    count, given = len(parts), sum(parts)
    blocks, both, outs = refs[:given], refs[given], refs[given + 1 : given + 1 + count]
    vx, vw, sems = refs[given + 1 + count :]
    spans = (pl.ds(0, SPLIT), pl.ds(SPLIT, both.shape[0] - SPLIT))
    weights = [
        pltpu.make_async_copy(both.at[span], vw.at[span], sems.at[n])
        for n, span in enumerate(spans)
    ]
    rows, n = [], 0
    for i, many in enumerate(parts):
        long = vx.shape[1] // many
        rows.append(
            [
                pltpu.make_async_copy(
                    blocks[n + j], vx.at[i, pl.ds(j * long, long)], sems.at[2 + n + j]
                )
                for j in range(many)
            ]
        )
        n += many
    for c in (*rows[0], *weights, *(c for group in rows[1:] for c in group)):
        c.start()
    for i, group in enumerate(rows):
        for c in group:
            c.wait()
        block = flat(vx.at[i])
        vals = None
        for span, c in zip(spans, weights, strict=True):
            if i == 0:
                c.wait()
            at, long = span.start, span.size
            term = jnp.dot(
                block[:, at : at + long], vw[at : at + long], preferred_element_type=F32
            )
            vals = term if vals is None else vals + term
        gate, up = jnp.split(vals, 2, axis=1)
        outs[i][...] = (gate * jax.nn.sigmoid(1.702 * gate) * (up + 1.0)).astype(BF16)


BANDS = [(0, 640), (640, 640), (1280, 640), (1920, 640), (2560, 320)]


def down_near_body(place, h0, h1, h3, shards, out):
    for at, long in BANDS:
        total = None
        for by, hid in ((0, h0), (1, h1), (3, h3)):
            shard = shards[lax.rem(place[1] + by, 4), at : at + long, :]
            term = lax.dot_general(hid[...], shard, NT, preferred_element_type=F32)
            total = term if by == 0 else total + term
        out[:, at : at + long] = total


def down_far_body(place, h2, near, shards, out):
    for at, long in BANDS:
        shard = shards[lax.rem(place[1] + 2, 4), at : at + long, :]
        total = near[:, at : at + long] + lax.dot_general(
            h2[...], shard, NT, preferred_element_type=F32
        )
        out[:, :, at : at + long] = total.reshape(out.shape[0], out.shape[1], long).astype(BF16)


def combine_body(stream, mix0, mix1, ret0, ret1, out):
    both = lax.dot_general(mix0[...], flat(ret0), TN, preferred_element_type=F32)
    both += lax.dot_general(mix1[...], flat(ret1), TN, preferred_element_type=F32)
    out[...] = (stream[...].astype(F32) + both[:64] + both[64:]).astype(BF16)


def shape(*dims, dtype=BF16):
    return jax.ShapeDtypeStruct(dims, dtype)


def per_device(
    queries,
    keys_values,
    hidden_in,
    out_weight,
    norm_gain,
    router_weight,
    expert_ids,
    expert_gate,
    expert_up,
    expert_down,
):
    tok_dev = queries.shape[0]
    rows_dev = hidden_in.shape[0]
    gate, up, down = expert_gate[0], expert_up[0], expert_down[0]
    width = gate.shape[1]
    owners = lax.axis_size("seq")
    rows = owners * PER

    def shift(a, by):
        return lax.ppermute(a, "fsdp", [(i, (i + by) % 4) for i in range(4)])

    downs = lax.all_gather(down, "fsdp", axis=0)
    key_rim = lax.ppermute(
        keys_values[tok_dev - WINDOW :], "seq", [(i, i + 1) for i in range(owners - 1)]
    )

    place = jnp.stack([lax.axis_index("seq"), lax.axis_index("fsdp")]).astype(jnp.int32)
    own, to1, to2, to3 = call(
        attention_body,
        (shape(rows_dev, D, dtype=F32),) + (shape(rows_dev, D),) * 3,
        [SMEM] + [VMEM] * 4,
        [pltpu.VMEM((tok_dev, queries.shape[1]), BF16)],
    )(place, queries, keys_values, key_rim, out_weight.T)
    r1, r2, r3 = shift(to1, 1), shift(to2, 2), shift(to3, 3)

    expert_ids, own = lax.optimization_barrier((expert_ids, own))
    chosen, *picks = call(
        routing_body,
        (shape(EXPERTS, rows_dev, dtype=F32),) + (shape(rows, rows_dev),) * CHUNKS,
        [VMEM],
    )(expert_ids.T)

    stream, normed, out0, out1 = call(
        norm_body,
        (shape(rows_dev, D),) * 2 + (shape(owners, PER, D),) * 2,
        [VMEM] * 8,
    )(own, r1, r2, r3, hidden_in, norm_gain[None, :], *picks)

    def exchange(a):
        return lax.all_to_all(a, "seq", split_axis=0, concat_axis=0, tiled=True)

    first = exchange(out0)
    out1, first = lax.optimization_barrier((out1, first))
    second = exchange(out1)
    mix0, mix1 = call(
        gates_body,
        (shape(rows, 2 * rows_dev),) * 2,
        [VMEM] * 5,
    )(normed, router_weight.T, chosen, *picks)

    half = owners // 2
    both = jnp.concatenate([gate, up], axis=1)

    def hidden(parts, *blocks):
        return call(
            functools.partial(hidden_body, parts),
            (shape(rows, width),) * len(parts),
            [ANY] * (sum(parts) + 1),
            [
                pltpu.VMEM((len(parts), owners, PER, D), BF16),
                pltpu.VMEM((D, 2 * width), BF16),
                pltpu.SemaphoreType.DMA((sum(parts) + 2,)),
            ],
        )(*blocks, both)

    def around(mine):
        low, high = mine[:half], mine[half:]
        return shift(low, 1), shift(high, -1), shift(high, 1), shift(low, -1)

    def near(mine, left_low, right_high, left_high, right_low):
        return hidden((1, 2, 2), mine, left_low, left_high, right_low, right_high)

    def opposite(left_low, right_high):
        return shift(left_low, 1), shift(right_high, -1)

    def back(hid_left, hid_right):
        return shift(hid_right, 1), shift(hid_left, -1)

    def answer(hid_own, from_left, from_right, from_far):
        near_sum = call(down_near_body, shape(rows, D, dtype=F32), [SMEM] + [VMEM] * 4)(
            place, hid_own, from_right, from_left, downs
        )
        return call(down_far_body, shape(owners, PER, D), [SMEM] + [VMEM] * 3)(
            place, from_far, near_sum, downs
        )

    beside = around(first)
    halves = opposite(*beside[:2])
    beside, downs, second = lax.optimization_barrier((beside, downs, second))
    low, high = second[:half], second[half:]
    own0, left0, right0 = near(first, *beside)
    halves, left0, right0 = lax.optimization_barrier((halves, left0, right0))
    (far0,) = hidden((2,), *halves)
    ready = shift(low, 1), shift(high, -1)
    moved = (*back(left0, right0), shift(far0, 2))
    low, high, moved, ready = lax.optimization_barrier((low, high, moved, ready))
    later = shift(high, 1), shift(low, -1)
    answer0 = answer(own0, *moved)
    answer0, ready, later = lax.optimization_barrier((answer0, ready, later))
    returned = [exchange(answer0)]
    own1, left1, right1 = near(second, *ready, *later)
    (far1,) = hidden((2,), *opposite(*ready))
    returned.append(exchange(answer(own1, *back(left1, right1), shift(far1, 2))))
    return call(
        combine_body,
        shape(rows_dev, D),
        [VMEM] * 5,
    )(stream, mix0, mix1, *returned)


def solution(mesh):
    return jax.shard_map(
        per_device,
        mesh=mesh,
        in_specs=(
            P("seq", "fsdp"),
            P("seq", "fsdp"),
            P(("seq", "fsdp"), None),
            P("fsdp", None),
            P(),
            P(),
            P(("seq", "fsdp"), None),
            P("seq", None, "fsdp"),
            P("seq", None, "fsdp"),
            P("seq", None, "fsdp"),
        ),
        out_specs=P(("seq", "fsdp"), None),
        check_vma=False,
    )
```
